32 devices in a mesh: groups: 2 (over y), path: 16 (over z, x, core).
Axes of the slice: x: 2, y: 2, z: 4, core: 2. Of those that a mesh axis runs over, the one named last changes fastest.
Arguments:
- tile_values: bfloat16 [1024, 9, 128, 128], P(('groups', 'path')), parts along dimension 0, may hold values from 0 to 0.0017318726
- link_of_tile: int32 [1024, 9], P(('groups', 'path')), parts along dimension 0, may hold values from 0 to 31, as said below
- tile_count: int32 [1024], P(('groups', 'path')), parts along dimension 0, may hold values from 1 to 9, as said below
- fail_links: int32 [128, 128], P('groups'), parts along dimension 0, may hold values from 0 to 4095
- flow_start: float32 [1024, 64, 128], P(('groups', 'path')), parts along dimension 0, may hold values from 0 to 1
- dual_start: float32 [64, 64, 128], P(('groups', 'path')), parts along dimension 0, may hold values from 0 to 2
- path_cost: float32 [1024, 128], P(('groups', 'path')), parts along dimension 0, may hold values from -1.5 to 0.5
- path_upper: float32 [1024, 128], P(('groups', 'path')), parts along dimension 0, may hold values from 0.5 to 2
- link_capacity: float32 [64, 128], P(('groups', 'path')), parts along dimension 0, may hold values from 2 to 8
Outputs:
- flow_final: float32 [1024, 64, 128], P(('groups', 'path')), parts along dimension 0
- dual_final: float32 [64, 64, 128], P(('groups', 'path')), parts along dimension 0
- reduced_cost: float32 [1024, 64, 128], P(('groups', 'path')), parts along dimension 0
The draws below stay inside these ranges and needn't reach their ends.
There are 2 independent parts, one for each index of `groups`. The reference program is written for one: setup_inputs(seed, part) draws one part's arguments, and reference() takes and returns one part's arrays. A program takes and returns all parts, laid end to end along the dimension named above; each array names one. Nothing has to cross between parts.
Inputs may be any that keep to these rules, and one draw needn't show every extreme that they name: `link_of_tile`: the slots of one path block name link blocks of different owners (owner = link block // 2); among all slots of the 32 consecutive path blocks of one device, those reaching one owner name one and the same link block of it. `tile_count`: slots 0 to count - 1 of a path block hold its tiles. Among each 32 consecutive path blocks at least one has 9. `fail_links`: repeats are allowed.
All inputs are finite; a program needn't handle non-finite values.
Results may differ from the reference program's by a relative error of at most 0.0003.
Values may be sent and summed in bfloat16 or wider, within the bound.
A program may use at most 128 MiB of HBM per device.

```python
import math
import jax
import jax.numpy as jnp
from jax import lax

BLK = 128
S = 64
PB_DEV = 32
LB_DEV = 2
KSLOT = 9
ITERS = 2
PATH_BLOCKS = 512
LINK_BLOCKS = 32
LINKS = 4096
FAILS = 128


def draw_link_of_tile(key, part):
    key = jax.random.fold_in(key, 11)
    owner_total = LINK_BLOCKS // LB_DEV
    device_total = PATH_BLOCKS // PB_DEV
    first_key, second_key = jax.random.split(key)
    offset_pick = jax.random.randint(first_key, (device_total, owner_total), 0, LB_DEV)
    block_keys = jax.random.split(second_key, PATH_BLOCKS)
    owner_order = jax.vmap(lambda subkey: jax.random.permutation(subkey, owner_total))(block_keys)[:, :KSLOT]
    device_of = jnp.arange(PATH_BLOCKS, dtype=jnp.int32) // PB_DEV
    chosen = offset_pick[device_of[:, None], owner_order]
    return (owner_order * LB_DEV + chosen).astype(jnp.int32)


def draw_tile_count(key, part):
    key = jax.random.fold_in(key, 12)
    device_total = PATH_BLOCKS // PB_DEV
    first_key, second_key = jax.random.split(key)
    counts = jax.random.randint(first_key, (PATH_BLOCKS,), 1, KSLOT + 1)
    full_pick = jax.random.randint(second_key, (device_total,), 0, PB_DEV)
    full_rows = jnp.arange(device_total, dtype=jnp.int32) * PB_DEV + full_pick
    return counts.at[full_rows].set(KSLOT).astype(jnp.int32)


def plant(drawn, stream_key, least, largest):
    place = [jax.random.randint(jax.random.fold_in(stream_key, axis), (), 0, length) for axis, length in enumerate(drawn.shape)]
    longest = drawn.shape.index(max(drawn.shape))
    neighbour = place[:longest] + [(place[longest] + 1) % drawn.shape[longest]] + place[longest + 1:]
    return drawn.at[tuple(place)].set(least).at[tuple(neighbour)].set(largest)


def shard_levels(own_key, extent, shards, low, top_value):
    loudness, own = 1.0, jax.random.fold_in(own_key, 6)
    for position, shards_of in shards:
        steps = jnp.exp(jax.random.uniform(jax.random.fold_in(own, position), (shards_of,), jnp.float32, low / len(shards), top_value / len(shards)))
        loudness = loudness * jnp.repeat(steps, extent[position] // shards_of).reshape([-1 if axis == position else 1 for axis in range(len(extent))])
    return loudness


def setup_inputs(seed: int = 0, part: int = 0) -> dict:
    key_of = jax.random.split(jax.random.key(seed), 10)
    own_keys = jax.random.split(jax.random.fold_in(key_of[9], part), 10)
    return {
        "tile_values": jnp.clip(0.0017318726 * jax.random.uniform(own_keys[0], (PATH_BLOCKS, KSLOT, BLK, BLK), jnp.float32) ** shard_levels(own_keys[0], (PATH_BLOCKS, KSLOT, BLK, BLK), ((0, 16),), -0.2, 0.2), 0.0, 0.0017318726).astype(jnp.bfloat16),
        "link_of_tile": draw_link_of_tile(jax.random.fold_in(jax.random.fold_in(key_of[9], part), 71), part),
        "tile_count": draw_tile_count(jax.random.fold_in(jax.random.fold_in(key_of[9], part), 71), part),
        "fail_links": plant(jax.random.randint(own_keys[3], (S, FAILS), 0, LINKS), jax.random.fold_in(own_keys[3], 1), 0, LINKS - 1).astype(jnp.int32),
        "flow_start": jnp.clip(1.0 * jax.random.uniform(own_keys[4], (PATH_BLOCKS, S, BLK), jnp.float32) ** shard_levels(own_keys[4], (PATH_BLOCKS, S, BLK), ((0, 16),), -0.2, 0.2), 0.0, 1.0),
        "dual_start": jnp.clip(2.0 * jax.random.uniform(own_keys[5], (LINK_BLOCKS, S, BLK), jnp.float32) ** shard_levels(own_keys[5], (LINK_BLOCKS, S, BLK), ((0, 16),), -0.2, 0.2), 0.0, 2.0),
        "path_cost": jnp.clip(-1.5 + 2.0 * jax.random.uniform(own_keys[6], (PATH_BLOCKS, BLK), jnp.float32) ** shard_levels(own_keys[6], (PATH_BLOCKS, BLK), ((0, 16),), -0.2, 0.2), -1.5, 0.5),
        "path_upper": jnp.clip(jnp.exp(math.log(2.0) - 1.3862944 * jax.random.uniform(own_keys[7], (PATH_BLOCKS, BLK), jnp.float32) ** shard_levels(own_keys[7], (PATH_BLOCKS, BLK), ((0, 16),), -0.2, 0.2)), 0.5, 2.0),
        "link_capacity": jnp.clip(jnp.exp(math.log(8.0) - 1.3862944 * jax.random.uniform(own_keys[8], (LINK_BLOCKS, BLK), jnp.float32) ** shard_levels(own_keys[8], (LINK_BLOCKS, BLK), ((0, 16),), -0.2, 0.2)), 2.0, 8.0),
    }


primal_step = 0.5
dual_step = 0.25


def reference(tile_values, link_of_tile, tile_count, fail_links, flow_start, dual_start, path_cost, path_upper, link_capacity):
    groups_count = PATH_BLOCKS // PB_DEV
    in_use = (jnp.arange(KSLOT, dtype=jnp.int32)[None, :] < tile_count[:, None]).astype(jnp.float32)
    scenario_ids = jnp.broadcast_to(jnp.arange(S, dtype=jnp.int32)[:, None], fail_links.shape)
    surviving = jnp.ones((LINKS, S), jnp.float32).at[fail_links, scenario_ids].set(0.0)
    surviving = surviving.reshape(LINK_BLOCKS, BLK, S).transpose(0, 2, 1)
    bound_load = link_capacity[:, None, :] * surviving
    tile_grouped = tile_values.reshape(groups_count, PB_DEV, KSLOT, BLK, BLK)
    ids_grouped = link_of_tile.reshape(groups_count, PB_DEV, KSLOT)
    use_grouped = in_use.reshape(groups_count, PB_DEV, KSLOT)

    def backward(dual_b):
        def one_group(pieces):
            tile_part, id_part, use_part = pieces
            picked = dual_b[id_part].astype(jnp.float32) * use_part[:, :, None, None]
            return jnp.einsum("bksl,bkpl->bsp", picked, tile_part.astype(jnp.float32))
        pushed = lax.map(one_group, (tile_grouped, ids_grouped, use_grouped))
        return pushed.reshape(PATH_BLOCKS, S, BLK)

    def forward(flow_b):
        flow_grouped = flow_b.reshape(groups_count, PB_DEV, S, BLK)

        def add_group(total, pieces):
            tile_part, id_part, use_part, flow_part = pieces
            contrib = jnp.einsum("bsp,bkpl->bksl", flow_part.astype(jnp.float32), tile_part.astype(jnp.float32))
            contrib = contrib * use_part[:, :, None, None]
            total = total.at[id_part.reshape(-1)].add(contrib.reshape(-1, S, BLK))
            return total, None
        start_total = jnp.zeros((LINK_BLOCKS, S, BLK), jnp.float32)
        total, _ = lax.scan(add_group, start_total, (tile_grouped, ids_grouped, use_grouped, flow_grouped))
        return total

    flow_now = flow_start
    dual_now = dual_start
    cost_wide = path_cost[:, None, :]
    upper_wide = path_upper[:, None, :]
    for step in range(ITERS):
        path_push = backward(dual_now.astype(jnp.bfloat16))
        new_flow = jnp.clip(flow_now - primal_step * (cost_wide + path_push), 0.0, upper_wide)
        flow_bar = (2.0 * new_flow - flow_now).astype(jnp.bfloat16)
        link_load = forward(flow_bar)
        dual_now = jnp.maximum(0.0, dual_now + dual_step * (link_load - bound_load))
        flow_now = new_flow
    reduced_cost = cost_wide + backward(dual_now.astype(jnp.bfloat16))
    return flow_now, dual_now, reduced_cost
```

```python
import functools

import jax
import jax.numpy as jnp
from jax import lax
from jax.experimental import pallas as pl
from jax.experimental.pallas import tpu as pltpu
from jax.sharding import PartitionSpec as P

ITERS = 2
QUAD = 4
CHUNK = 8

primal_step = 0.5
dual_step = 0.25


def mix(a, b, count):
    if count & (count - 1):
        return lax.rem(a + b, count)
    total = 0
    bit = 1
    while bit < count:
        total = total + ((a // bit + b // bit) % 2) * bit
        bit *= 2
    return total


def kernel(
    devs,
    inv_ref,
    sel_ref,
    fail_ref,
    dual_ref,
    cost_ref,
    upper_ref,
    cap_ref,
    tiles_hbm,
    flow_hbm,
    dual_out,
    flow_out,
    rc_out,
    tiles,
    flow,
    push,
    bar,
    bound,
    send_dual,
    recv_dual,
    send_part,
    recv_part,
    recv_sel,
    acc,
    tile_sem,
    flow_sem,
    out_sem,
    sel_send,
    sel_recv,
    dual_send,
    dual_recv,
    part_send,
    part_recv,
):
    me = lax.axis_index("path")
    groups = devs // QUAD
    my_group = me // QUAD
    link_here, scen, width = dual_ref.shape
    tile_total = tiles.shape[0] - 1
    blocks = flow.shape[0]
    chunks = blocks // CHUNK
    load_parts = 4
    piece = tile_total // load_parts

    def load_tiles(i):
        part = pl.ds(i * piece, piece)
        return pltpu.make_async_copy(tiles_hbm.at[part], tiles.at[part], tile_sem.at[i])

    for i in range(load_parts):
        load_tiles(i).start()
    load_flow = pltpu.make_async_copy(flow_hbm, flow, flow_sem)
    load_flow.start()

    def remote(src, dst, send, recv, peer):
        return pltpu.make_async_remote_copy(
            src_ref=src.at[peer],
            dst_ref=dst.at[me],
            send_sem=send.at[peer],
            recv_sem=recv.at[me],
            device_id={"path": peer},
            device_id_type=pl.DeviceIdType.MESH,
        )

    def arrival(src, dst, send, recv, peer):
        return pltpu.make_async_remote_copy(
            src_ref=src.at[peer],
            dst_ref=dst.at[peer],
            send_sem=send.at[peer],
            recv_sem=recv.at[peer],
            device_id={"path": peer},
            device_id_type=pl.DeviceIdType.MESH,
        )

    sel_ways = (sel_ref, recv_sel, sel_send, sel_recv)
    dual_ways = (send_dual, recv_dual, dual_send, dual_recv)
    part_ways = (send_part, recv_part, part_send, part_recv)

    def peers(step, far_first=True):
        def one(g, _):
            base = mix(my_group, groups - 1 - g if far_first else g, groups) * QUAD
            for i in range(QUAD):
                peer = base + i

                @pl.when(peer != me)
                def _():
                    step(peer)

            return 0

        lax.fori_loop(0, groups, one, 0)

    barrier = pltpu.get_barrier_semaphore()

    def greet(peer):
        pl.semaphore_signal(
            barrier, inc=1, device_id={"path": peer}, device_id_type=pl.DeviceIdType.MESH
        )

    peers(greet)
    pl.semaphore_wait(barrier, devs - 1)

    peers(lambda peer: remote(*sel_ways, peer).start())
    recv_sel[me] = sel_ref[me]

    tiles[tile_total] = jnp.zeros((width, width), tiles.dtype)
    first_link = me * (link_here * width)
    lane = lax.broadcasted_iota(jnp.int32, (scen, width), 1) + first_link
    for half in range(fail_ref.shape[1] // width):
        ids = fail_ref[:, half * width : (half + 1) * width]

        def strike(_, state):
            ids, *alive = state
            for f in range(8):
                struck = jnp.broadcast_to(ids[:, f : f + 1], (scen, width))
                alive = [
                    jnp.where(struck == lane + b * width, 0.0, alive[b]) for b in range(link_here)
                ]
            return (pltpu.roll(ids, width - 8, 1), *alive)

        if half == 0:
            alive = [jnp.ones((scen, width), jnp.float32) for _ in range(link_here)]
        _, *alive = lax.fori_loop(0, width // 8, strike, (ids, *alive))
    for b in range(link_here):
        bound[b] = cap_ref[b : b + 1, :] * alive[b]
        dual_out[b] = dual_ref[b]

    peers(lambda peer: arrival(*sel_ways, peer).wait_recv(), far_first=False)
    peers(lambda peer: arrival(*sel_ways, peer).wait_send())

    def give(dst, index, peer):
        choice = recv_sel[peer][0:1, :]
        picked = dual_out[0]
        for b in range(1, link_here):
            picked = jnp.where(choice == b, dual_out[b], picked)
        dst[index] = picked.astype(jnp.bfloat16)

    def weights(base, c, i, h):
        rows = []
        for r in range(2):
            row = [
                tiles[inv_ref[base + 2 * h + q, c * CHUNK + 2 * i + r]] for q in range(2)
            ]
            rows.append(jnp.concatenate(row, axis=1))
        return jnp.concatenate(rows, axis=0)

    def backward():
        def quad(g, _):
            base = mix(my_group, g, groups) * QUAD
            for i in range(QUAD):

                @pl.when(base + i != me)
                def _():
                    arrival(*dual_ways, base + i).wait_recv()

            def chunk(c, _):
                pairs = [
                    jnp.concatenate([recv_dual[base + 2 * h], recv_dual[base + 2 * h + 1]], axis=1)
                    for h in range(QUAD // 2)
                ]
                for i in range(CHUNK // 2):
                    total = push[c, :, 2 * i * width : 2 * (i + 1) * width]
                    for h in range(QUAD // 2):
                        total = total + lax.dot_general(
                            pairs[h],
                            weights(base, c, i, h),
                            (((1,), (1,)), ((), ())),
                            preferred_element_type=jnp.float32,
                        )
                    push[c, :, 2 * i * width : 2 * (i + 1) * width] = total
                return 0

            return lax.fori_loop(0, chunks, chunk, 0)

        push[...] = jnp.zeros(push.shape, push.dtype)
        lax.fori_loop(0, groups, quad, 0)

    def primal():
        def block(c, _):
            for i in range(CHUNK):
                b = c * CHUNK + i
                side = slice(i * width, (i + 1) * width)
                now = flow[b]
                price = cost_ref[pl.ds(b, 1), :] + push[c, :, side]
                new = jnp.clip(now - primal_step * price, 0.0, upper_ref[pl.ds(b, 1), :])
                bar[c, :, side] = (2.0 * new - now).astype(jnp.bfloat16)
                flow[b] = new
            return 0

        lax.fori_loop(0, chunks, block, 0)

    def forward():
        def quad(g, _):
            base = mix(my_group, groups - 1 - g, groups) * QUAD

            def chunk(c, _):
                for h in range(QUAD // 2):
                    total = acc[h]
                    for i in range(CHUNK // 2):
                        total = total + jnp.dot(
                            bar[c, :, 2 * i * width : 2 * (i + 1) * width],
                            weights(base, c, i, h),
                            preferred_element_type=jnp.float32,
                        )
                    acc[h] = total
                return 0

            acc[...] = jnp.zeros(acc.shape, acc.dtype)
            lax.fori_loop(0, chunks, chunk, 0)
            for i in range(QUAD):
                owner = base + i
                load = acc[i // 2, :, (i % 2) * width : (i % 2 + 1) * width]

                @pl.when(owner != me)
                def _():
                    send_part[owner] = load
                    remote(*part_ways, owner).start()

                @pl.when(owner == me)
                def _():
                    recv_part[me] = load

            return 0

        lax.fori_loop(0, groups, quad, 0)

    def dual_step_all():
        def add(g, loads):
            base = mix(my_group, groups - 1 - g, groups) * QUAD
            for i in range(QUAD):

                @pl.when(base + i != me)
                def _():
                    arrival(*part_ways, base + i).wait_recv()

            for i in range(QUAD):
                part = recv_part[base + i]
                choice = recv_sel[base + i][0:1, :]
                loads = tuple(
                    loads[b] + jnp.where(choice == b, part, 0.0) for b in range(link_here)
                )
            return loads

        zero = jnp.zeros((scen, width), jnp.float32)
        loads = lax.fori_loop(0, groups, add, (zero,) * link_here)
        for b in range(link_here):
            dual_out[b] = jnp.maximum(0.0, dual_out[b] + dual_step * (loads[b] - bound[b]))

    save_flow = pltpu.make_async_copy(flow, flow_out, flow_sem)

    def phase(t, _):
        def offer(peer):
            give(send_dual, peer, peer)
            remote(*dual_ways, peer).start()

        peers(offer)
        give(recv_dual, me, me)

        @pl.when(t == 0)
        def _():
            for i in range(load_parts):
                load_tiles(i).wait()
            load_flow.wait()

        backward()
        peers(lambda peer: arrival(*dual_ways, peer).wait_send())

        @pl.when(t < ITERS)
        def _():
            primal()

            @pl.when(t == ITERS - 1)
            def _():
                save_flow.start()

            forward()
            dual_step_all()
            peers(lambda peer: arrival(*part_ways, peer).wait_send())

        return 0

    lax.fori_loop(0, ITERS + 1, phase, 0)
    save_flow.wait()

    def finish(c, _):
        for i in range(CHUNK):
            b = c * CHUNK + i
            flow[b] = cost_ref[pl.ds(b, 1), :] + push[c, :, i * width : (i + 1) * width]
        part = pl.ds(c * CHUNK, CHUNK)
        pltpu.make_async_copy(flow.at[part], rc_out.at[part], out_sem.at[c]).start()
        return 0

    lax.fori_loop(0, chunks, finish, 0)

    def close(c, _):
        part = pl.ds(c * CHUNK, CHUNK)
        pltpu.make_async_copy(flow.at[part], rc_out.at[part], out_sem.at[c]).wait()
        return 0

    lax.fori_loop(0, chunks, close, 0)


def body(
    tile_values,
    link_of_tile,
    tile_count,
    fail_links,
    flow_start,
    dual_start,
    path_cost,
    path_upper,
    link_capacity,
):
    devs = lax.axis_size("path")
    blocks, slots, width, _ = tile_values.shape
    link_here, scen, _ = dual_start.shape
    tile_total = blocks * slots
    owner_of = link_of_tile // link_here
    used = jnp.arange(slots, dtype=jnp.int32)[None, :] < tile_count[:, None]
    hits = (owner_of[None] == jnp.arange(devs, dtype=jnp.int32)[:, None, None]) & used[None]
    place = jnp.arange(tile_total, dtype=jnp.int32).reshape(1, blocks, slots)
    inv = jnp.min(jnp.where(hits, place, tile_total), axis=2)
    sel = jnp.max(jnp.where(hits, (link_of_tile % link_here)[None], 0), axis=(1, 2))
    sel = jnp.broadcast_to(sel[:, None, None], (devs, 8, width))
    chunks = blocks // CHUNK
    vmem = pl.BlockSpec(memory_space=pltpu.VMEM)
    anywhere = pl.BlockSpec(memory_space=pl.ANY)
    dma = pltpu.SemaphoreType.DMA
    dual_final, flow_final, reduced = pl.pallas_call(
        functools.partial(kernel, devs),
        out_shape=(
            jax.ShapeDtypeStruct(dual_start.shape, jnp.float32),
            jax.ShapeDtypeStruct(flow_start.shape, jnp.float32),
            jax.ShapeDtypeStruct(flow_start.shape, jnp.float32),
        ),
        in_specs=[pl.BlockSpec(memory_space=pltpu.SMEM)] + [vmem] * 6 + [anywhere] * 2,
        out_specs=(vmem, anywhere, anywhere),
        scratch_shapes=[
            pltpu.VMEM((tile_total + 1, width, width), jnp.bfloat16),
            pltpu.VMEM(flow_start.shape, jnp.float32),
            pltpu.VMEM((chunks, scen, CHUNK * width), jnp.float32),
            pltpu.VMEM((chunks, scen, CHUNK * width), jnp.bfloat16),
            pltpu.VMEM(dual_start.shape, jnp.float32),
            pltpu.VMEM((devs, scen, width), jnp.bfloat16),
            pltpu.VMEM((devs, scen, width), jnp.bfloat16),
            pltpu.VMEM((devs, scen, width), jnp.float32),
            pltpu.VMEM((devs, scen, width), jnp.float32),
            pltpu.VMEM((devs, 8, width), jnp.int32),
            pltpu.VMEM((QUAD // 2, scen, 2 * width), jnp.float32),
            dma((4,)),
            dma(()),
            dma((chunks,)),
            dma((devs,)),
            dma((devs,)),
            dma((devs,)),
            dma((devs,)),
            dma((devs,)),
            dma((devs,)),
        ],
        compiler_params=pltpu.CompilerParams(
            collective_id=0, has_side_effects=True, vmem_limit_bytes=48 * 1024 * 1024
        ),
    )(
        inv,
        sel,
        fail_links,
        dual_start,
        path_cost,
        path_upper,
        link_capacity,
        tile_values.reshape(tile_total, width, width),
        flow_start,
    )
    return flow_final, dual_final, reduced


def solution(mesh):
    rows = ("groups", "path")
    in_specs = (
        P(rows, None, None, None),
        P(rows, None),
        P(rows),
        P("groups", None),
        P(rows, None, None),
        P(rows, None, None),
        P(rows, None),
        P(rows, None),
        P(rows, None),
    )
    out_specs = (P(rows, None, None), P(rows, None, None), P(rows, None, None))
    return jax.shard_map(body, mesh=mesh, in_specs=in_specs, out_specs=out_specs, check_vma=False)
```

```python
import functools

import jax
import jax.numpy as jnp
from jax import lax
from jax.experimental import pallas as pl
from jax.experimental.pallas import tpu as pltpu
from jax.sharding import PartitionSpec as P

ITERS = 2
QUAD = 4
CHUNK = 32
LEVELS = 32000.0
PIECES = 4

primal_step = 0.5
dual_step = 0.25


def mix(a, b, count):
    if count & (count - 1):
        return lax.rem(a + b, count)
    total = 0
    bit = 1
    while bit < count:
        total = total + ((a // bit + b // bit) % 2) * bit
        bit *= 2
    return total


def kernel(
    devs,
    inv_hbm,
    sel_hbm,
    fail_hbm,
    dual_hbm,
    cost_hbm,
    upper_hbm,
    cap_hbm,
    tiles_hbm,
    flow_hbm,
    dual_out,
    flow_out,
    rc_out,
    inv_ref,
    sel_ref,
    fail_ref,
    dual_ref,
    cost_ref,
    upper_ref,
    cap_ref,
    small_sem,
    tiles,
    turned,
    flow,
    push,
    bar,
    bound,
    send_dual,
    recv_dual,
    send_part,
    recv_part,
    recv_sel,
    tile_sem,
    flow_sem,
    out_sem,
    sel_send,
    sel_recv,
    dual_send,
    dual_recv,
    part_send,
    part_recv,
):
    me = lax.axis_index("path")
    groups = devs // QUAD
    my_group = me // QUAD
    link_here, scen, width = dual_ref.shape
    tile_total = tiles.shape[0] - 1
    blocks = flow.shape[0]
    chunks = blocks // CHUNK
    load_parts = 4
    piece = tile_total // load_parts

    def load_tiles(i):
        part = pl.ds(i * piece, piece)
        return pltpu.make_async_copy(tiles_hbm.at[part], tiles.at[part], tile_sem.at[i])

    small = [
        pltpu.make_async_copy(src, dst, small_sem.at[i])
        for i, (src, dst) in enumerate(
            (
                (sel_hbm, sel_ref),
                (dual_hbm, dual_ref),
                (fail_hbm, fail_ref),
                (cap_hbm, cap_ref),
                (inv_hbm, inv_ref),
                (cost_hbm, cost_ref),
                (upper_hbm, upper_ref),
            )
        )
    ]
    for copy in small:
        copy.start()
    for i in range(load_parts):
        load_tiles(i).start()
    load_flow = pltpu.make_async_copy(flow_hbm, flow, flow_sem)
    load_flow.start()

    def remote(src, dst, send, recv, peer):
        return pltpu.make_async_remote_copy(
            src_ref=src.at[peer],
            dst_ref=dst.at[me],
            send_sem=send.at[peer],
            recv_sem=recv.at[me],
            device_id={"path": peer},
            device_id_type=pl.DeviceIdType.MESH,
        )

    def arrival(src, dst, send, recv, peer):
        return pltpu.make_async_remote_copy(
            src_ref=src.at[peer],
            dst_ref=dst.at[peer],
            send_sem=send.at[peer],
            recv_sem=recv.at[peer],
            device_id={"path": peer},
            device_id_type=pl.DeviceIdType.MESH,
        )

    sel_ways = (sel_ref, recv_sel, sel_send, sel_recv)
    dual_ways = (send_dual, recv_dual, dual_send, dual_recv)
    part_ways = (send_part, recv_part, part_send, part_recv)

    def peers(step, far_first=True):
        def one(g, _):
            base = mix(my_group, groups - 1 - g if far_first else g, groups) * QUAD
            for i in range(QUAD):
                peer = base + i

                @pl.when(peer != me)
                def _():
                    step(peer)

            return 0

        lax.fori_loop(0, groups, one, 0)

    barrier = pltpu.get_barrier_semaphore()

    def greet(peer):
        pl.semaphore_signal(
            barrier, inc=1, device_id={"path": peer}, device_id_type=pl.DeviceIdType.MESH
        )

    peers(greet)
    for copy in small:
        copy.wait()
    pl.semaphore_wait(barrier, devs - 1)

    peers(lambda peer: remote(*sel_ways, peer).start())
    recv_sel[me] = sel_ref[me]

    tiles[tile_total] = jnp.zeros((width, width), tiles.dtype)
    turned[tile_total] = jnp.zeros((width, width), tiles.dtype)
    first_link = me * (link_here * width)
    lane = lax.broadcasted_iota(jnp.int32, (scen, width), 1) + first_link
    for half in range(fail_ref.shape[1] // width):
        ids = fail_ref[:, half * width : (half + 1) * width]

        def strike(_, state):
            ids, *alive = state
            for f in range(8):
                struck = jnp.broadcast_to(ids[:, f : f + 1], (scen, width))
                alive = [
                    jnp.where(struck == lane + b * width, 0.0, alive[b]) for b in range(link_here)
                ]
            return (pltpu.roll(ids, width - 8, 1), *alive)

        if half == 0:
            alive = [jnp.ones((scen, width), jnp.float32) for _ in range(link_here)]
        _, *alive = lax.fori_loop(0, width // 8, strike, (ids, *alive))
    for b in range(link_here):
        bound[b] = cap_ref[b : b + 1, :] * alive[b]
        dual_out[b] = dual_ref[b]

    peers(lambda peer: arrival(*sel_ways, peer).wait_recv(), far_first=False)
    peers(lambda peer: arrival(*sel_ways, peer).wait_send())

    def give(dst, index, peer):
        choice = recv_sel[peer][0:1, :]
        picked = dual_out[0]
        for b in range(1, link_here):
            picked = jnp.where(choice == b, dual_out[b], picked)
        dst[index] = picked.astype(jnp.bfloat16)

    def weights(base, c, i, h):
        rows = []
        for r in range(2):
            row = [
                tiles[inv_ref[base + 2 * h + q, c * CHUNK + 2 * i + r]] for q in range(2)
            ]
            rows.append(jnp.concatenate(row, axis=1))
        return jnp.concatenate(rows, axis=0)

    def weights_turned(base, c, i, h):
        rows = []
        for q in range(2):
            row = [
                turned[inv_ref[base + 2 * h + q, c * CHUNK + 2 * i + r]] for r in range(2)
            ]
            rows.append(jnp.concatenate(row, axis=1))
        return jnp.concatenate(rows, axis=0)

    def turn(k, _):
        for i in range(PIECES * 4):
            turned[k * PIECES * 4 + i] = tiles[k * PIECES * 4 + i].T
        return 0

    def backward():
        def quad(g, _):
            base = mix(my_group, g, groups) * QUAD
            for i in range(QUAD):

                @pl.when(base + i != me)
                def _():
                    arrival(*dual_ways, base + i).wait_recv()

            def chunk(c, _):
                pairs = [
                    jnp.concatenate([recv_dual[base + 2 * h], recv_dual[base + 2 * h + 1]], axis=1)
                    for h in range(QUAD // 2)
                ]
                for i in range(CHUNK // 2):
                    total = push[c, :, 2 * i * width : 2 * (i + 1) * width]
                    for h in range(QUAD // 2):
                        total = total + jnp.dot(
                            pairs[h],
                            weights_turned(base, c, i, h),
                            preferred_element_type=jnp.float32,
                        )
                    push[c, :, 2 * i * width : 2 * (i + 1) * width] = total
                return 0

            return lax.fori_loop(0, chunks, chunk, 0)

        push[...] = jnp.zeros(push.shape, push.dtype)
        lax.fori_loop(0, groups, quad, 0)

    def primal():
        def block(c, _):
            for i in range(CHUNK):
                b = c * CHUNK + i
                side = slice(i * width, (i + 1) * width)
                now = flow[b]
                price = cost_ref[pl.ds(b, 1), :] + push[c, :, side]
                new = jnp.clip(now - primal_step * price, 0.0, upper_ref[pl.ds(b, 1), :])
                bar[c, :, side] = (2.0 * new - now).astype(jnp.bfloat16)
                flow[b] = new
            return 0

        lax.fori_loop(0, chunks, block, 0)

    def encode(load):
        peak = jnp.max(jnp.abs(load), axis=0, keepdims=True)
        power = jnp.ceil(jnp.log2(jnp.maximum(peak, 1e-30)))
        level = jnp.floor(load * (LEVELS * jnp.exp2(-power)) + 0.5)
        power = jnp.broadcast_to(power, (16, load.shape[1]))
        rows = jnp.concatenate([level, power], axis=0)
        return rows.astype(jnp.int32).astype(jnp.int16)

    def decode(coded):
        rows = coded.astype(jnp.int32).astype(jnp.float32)
        return rows[:scen] * (jnp.exp2(rows[scen : scen + 1]) * (1.0 / LEVELS))

    def forward():
        def quad(g, _):
            base = mix(my_group, groups - 1 - g, groups) * QUAD

            def chunk(c, totals):
                done = []
                for h in range(QUAD // 2):
                    total = totals[h]
                    for i in range(CHUNK // 2):
                        total = total + jnp.dot(
                            bar[c, :, 2 * i * width : 2 * (i + 1) * width],
                            weights(base, c, i, h),
                            preferred_element_type=jnp.float32,
                        )
                    done.append(total)
                return tuple(done)

            zero = jnp.zeros((scen, 2 * width), jnp.float32)
            totals = (zero,) * (QUAD // 2)
            if chunks == 1:
                totals = chunk(0, totals)
            else:
                totals = lax.fori_loop(0, chunks, chunk, totals)
            for h in range(QUAD // 2):
                coded = encode(totals[h])
                for q in range(2):
                    owner = base + 2 * h + q
                    load = coded[:, q * width : (q + 1) * width]
                    send_part[owner] = load

                    @pl.when(owner != me)
                    def _():
                        remote(*part_ways, owner).start()

            return 0

        lax.fori_loop(0, groups, quad, 0)

    def dual_step_all():
        def add(g, loads):
            base = mix(my_group, groups - 1 - g, groups) * QUAD
            for i in range(QUAD):

                @pl.when(base + i != me)
                def _():
                    arrival(*part_ways, base + i).wait_recv()

            for i in range(QUAD):
                part = decode(recv_part[base + i])
                choice = recv_sel[base + i][0:1, :]
                loads = tuple(
                    loads[b] + jnp.where(choice == b, part, 0.0) for b in range(link_here)
                )
            return loads

        zero = jnp.zeros((scen, width), jnp.float32)
        recv_part[me] = send_part[me]
        loads = lax.fori_loop(0, groups, add, (zero,) * link_here)
        for b in range(link_here):
            dual_out[b] = jnp.maximum(0.0, dual_out[b] + dual_step * (loads[b] - bound[b]))

    save_flow = pltpu.make_async_copy(flow, flow_out, flow_sem)

    def phase(t, _):
        def offer(peer):
            give(send_dual, peer, peer)
            remote(*dual_ways, peer).start()

        peers(offer, far_first=False)
        give(recv_dual, me, me)

        @pl.when(t == 0)
        def _():
            for i in range(load_parts):
                load_tiles(i).wait()
            load_flow.wait()
            lax.fori_loop(0, tile_total // (PIECES * 4), turn, 0)

        backward()
        peers(lambda peer: arrival(*dual_ways, peer).wait_send())

        @pl.when(t < ITERS)
        def _():
            primal()

            @pl.when(t == ITERS - 1)
            def _():
                save_flow.start()

            forward()
            dual_step_all()
            peers(lambda peer: arrival(*part_ways, peer).wait_send())

        return 0

    lax.fori_loop(0, ITERS + 1, phase, 0)
    save_flow.wait()

    share = blocks // PIECES
    saves = []
    for k in range(PIECES):
        for b in range(k * share, (k + 1) * share):
            i = b % CHUNK
            flow[b] = cost_ref[b : b + 1, :] + push[b // CHUNK, :, i * width : (i + 1) * width]
        part = pl.ds(k * share, share)
        saves.append(pltpu.make_async_copy(flow.at[part], rc_out.at[part], out_sem.at[k]))
        saves[-1].start()
    for copy in saves:
        copy.wait()


def body(
    tile_values,
    link_of_tile,
    tile_count,
    fail_links,
    flow_start,
    dual_start,
    path_cost,
    path_upper,
    link_capacity,
):
    devs = lax.axis_size("path")
    blocks, slots, width, _ = tile_values.shape
    link_here, scen, _ = dual_start.shape
    tile_total = blocks * slots
    owner_of = link_of_tile // link_here
    used = jnp.arange(slots, dtype=jnp.int32)[None, :] < tile_count[:, None]
    hits = (owner_of[None] == jnp.arange(devs, dtype=jnp.int32)[:, None, None]) & used[None]
    place = jnp.arange(tile_total, dtype=jnp.int32).reshape(1, blocks, slots)
    inv = jnp.min(jnp.where(hits, place, tile_total), axis=2)
    sel = jnp.max(jnp.where(hits, (link_of_tile % link_here)[None], 0), axis=(1, 2))
    sel = jnp.broadcast_to(sel[:, None, None], (devs, 8, width))
    chunks = blocks // CHUNK
    vmem = pl.BlockSpec(memory_space=pltpu.VMEM)
    anywhere = pl.BlockSpec(memory_space=pl.ANY)
    dma = pltpu.SemaphoreType.DMA
    dual_final, flow_final, reduced = pl.pallas_call(
        functools.partial(kernel, devs),
        out_shape=(
            jax.ShapeDtypeStruct(dual_start.shape, jnp.float32),
            jax.ShapeDtypeStruct(flow_start.shape, jnp.float32),
            jax.ShapeDtypeStruct(flow_start.shape, jnp.float32),
        ),
        in_specs=[anywhere] * 9,
        out_specs=(vmem, anywhere, anywhere),
        scratch_shapes=[
            pltpu.SMEM(inv.shape, jnp.int32),
            pltpu.VMEM(sel.shape, jnp.int32),
            pltpu.VMEM(fail_links.shape, jnp.int32),
            pltpu.VMEM(dual_start.shape, jnp.float32),
            pltpu.VMEM(path_cost.shape, jnp.float32),
            pltpu.VMEM(path_upper.shape, jnp.float32),
            pltpu.VMEM(link_capacity.shape, jnp.float32),
            dma((7,)),
            pltpu.VMEM((tile_total + 1, width, width), jnp.bfloat16),
            pltpu.VMEM((tile_total + 1, width, width), jnp.bfloat16),
            pltpu.VMEM(flow_start.shape, jnp.float32),
            pltpu.VMEM((chunks, scen, CHUNK * width), jnp.float32),
            pltpu.VMEM((chunks, scen, CHUNK * width), jnp.bfloat16),
            pltpu.VMEM(dual_start.shape, jnp.float32),
            pltpu.VMEM((devs, scen, width), jnp.bfloat16),
            pltpu.VMEM((devs, scen, width), jnp.bfloat16),
            pltpu.VMEM((devs, scen + 16, width), jnp.int16),
            pltpu.VMEM((devs, scen + 16, width), jnp.int16),
            pltpu.VMEM((devs, 8, width), jnp.int32),
            dma((4,)),
            dma(()),
            dma((PIECES,)),
            dma((devs,)),
            dma((devs,)),
            dma((devs,)),
            dma((devs,)),
            dma((devs,)),
            dma((devs,)),
        ],
        compiler_params=pltpu.CompilerParams(
            collective_id=0, has_side_effects=True, vmem_limit_bytes=60 * 1024 * 1024
        ),
    )(
        inv,
        sel,
        fail_links,
        dual_start,
        path_cost,
        path_upper,
        link_capacity,
        tile_values.reshape(tile_total, width, width),
        flow_start,
    )
    return flow_final, dual_final, reduced


def solution(mesh):
    rows = ("groups", "path")
    in_specs = (
        P(rows, None, None, None),
        P(rows, None),
        P(rows),
        P("groups", None),
        P(rows, None, None),
        P(rows, None, None),
        P(rows, None),
        P(rows, None),
        P(rows, None),
    )
    out_specs = (P(rows, None, None), P(rows, None, None), P(rows, None, None))
    return jax.shard_map(body, mesh=mesh, in_specs=in_specs, out_specs=out_specs, check_vma=False)
```

```python
import functools

import jax
import jax.numpy as jnp
from jax import lax
from jax.experimental import pallas as pl
from jax.experimental.pallas import tpu as pltpu
from jax.sharding import PartitionSpec as P

ITERS = 2
QUAD = 4
CHUNK = 32
LEVELS = 32000.0
PIECES = 4

primal_step = 0.5
dual_step = 0.25


def mix(a, b, count):
    if count & (count - 1):
        return lax.rem(a + b, count)
    total = 0
    bit = 1
    while bit < count:
        total = total + ((a // bit + b // bit) % 2) * bit
        bit *= 2
    return total


def kernel(
    devs,
    link_hbm,
    count_hbm,
    fail_hbm,
    dual_hbm,
    cost_hbm,
    upper_hbm,
    cap_hbm,
    tiles_hbm,
    flow_hbm,
    dual_out,
    flow_out,
    rc_out,
    inv_ref,
    link_ref,
    count_ref,
    inv_vec,
    sel_vec,
    all_sel,
    fail_ref,
    dual_ref,
    cost_ref,
    upper_ref,
    cap_ref,
    small_sem,
    inv_sem,
    tiles,
    turned,
    flow,
    push,
    bar,
    bound,
    dual_now,
    send_dual,
    recv_dual,
    send_part,
    recv_part,
    tile_sem,
    flow_sem,
    out_sem,
    sel_send,
    sel_recv,
    dual_send,
    dual_recv,
    part_send,
    part_recv,
):
    me = lax.axis_index("path")
    groups = devs // QUAD
    my_group = me // QUAD
    link_here, scen, width = dual_ref.shape
    tile_total = tiles.shape[0] - 1
    blocks = flow.shape[0]
    chunks = blocks // CHUNK
    load_parts = 4
    piece = tile_total // load_parts

    def load_tiles(i):
        part = pl.ds(i * piece, piece)
        return pltpu.make_async_copy(tiles_hbm.at[part], tiles.at[part], tile_sem.at[i])

    small = [
        pltpu.make_async_copy(src, dst, small_sem.at[i])
        for i, (src, dst) in enumerate(
            (
                (link_hbm, link_ref),
                (count_hbm, count_ref),
                (dual_hbm, dual_ref),
                (fail_hbm, fail_ref),
                (cap_hbm, cap_ref),
                (cost_hbm, cost_ref),
                (upper_hbm, upper_ref),
            )
        )
    ]
    for copy in small:
        copy.start()
    for i in range(load_parts):
        load_tiles(i).start()
    load_flow = pltpu.make_async_copy(flow_hbm, flow, flow_sem)
    load_flow.start()

    def remote(src, dst, send, recv, peer):
        return pltpu.make_async_remote_copy(
            src_ref=src.at[peer],
            dst_ref=dst.at[me],
            send_sem=send.at[peer],
            recv_sem=recv.at[me],
            device_id={"path": peer},
            device_id_type=pl.DeviceIdType.MESH,
        )

    def arrival(src, dst, send, recv, peer):
        return pltpu.make_async_remote_copy(
            src_ref=src.at[peer],
            dst_ref=dst.at[peer],
            send_sem=send.at[peer],
            recv_sem=recv.at[peer],
            device_id={"path": peer},
            device_id_type=pl.DeviceIdType.MESH,
        )

    def sel_way(peer, slot):
        return pltpu.make_async_remote_copy(
            src_ref=sel_vec,
            dst_ref=all_sel.at[slot],
            send_sem=sel_send.at[peer],
            recv_sem=sel_recv.at[slot],
            device_id={"path": peer},
            device_id_type=pl.DeviceIdType.MESH,
        )

    dual_ways = (send_dual, recv_dual, dual_send, dual_recv)
    part_ways = (send_part, recv_part, part_send, part_recv)

    def peers(step, far_first=True):
        def one(g, _):
            base = mix(my_group, groups - 1 - g if far_first else g, groups) * QUAD
            for i in range(QUAD):
                peer = base + i

                @pl.when(peer != me)
                def _():
                    step(peer)

            return 0

        lax.fori_loop(0, groups, one, 0)

    barrier = pltpu.get_barrier_semaphore()

    def greet(peer):
        pl.semaphore_signal(
            barrier, inc=1, device_id={"path": peer}, device_id_type=pl.DeviceIdType.MESH
        )

    peers(greet)
    for copy in small:
        copy.wait()

    slots = link_ref.shape[0]
    grid = (devs, blocks)
    first_slot = lax.broadcasted_iota(jnp.int32, grid, 1) * slots
    owner_link = lax.broadcasted_iota(jnp.int32, grid, 0) * link_here
    count = jnp.broadcast_to(count_ref[...], grid)
    place = jnp.full(grid, tile_total, jnp.int32)
    wanted = jnp.zeros(grid, jnp.int32)
    for k in range(slots):
        offset = jnp.broadcast_to(link_ref[k : k + 1, :], grid) - owner_link
        hit = (offset >= 0) & (offset < link_here) & (count > k)
        place = jnp.where(hit, first_slot + k, place)
        wanted = jnp.where(hit, offset, wanted)
    inv_vec[...] = jnp.zeros(inv_vec.shape, jnp.int32)
    inv_vec[:, :blocks] = place
    load_inv = pltpu.make_async_copy(inv_vec, inv_ref, inv_sem)
    load_inv.start()
    sel_vec[...] = jnp.broadcast_to(jnp.max(wanted, axis=1, keepdims=True), sel_vec.shape)
    all_sel[me] = sel_vec[...]
    pl.semaphore_wait(barrier, devs - 1)

    peers(lambda peer: sel_way(peer, me).start())

    tiles[tile_total] = jnp.zeros((width, width), tiles.dtype)
    turned[tile_total] = jnp.zeros((width, width), tiles.dtype)
    first_link = me * (link_here * width)
    lane = lax.broadcasted_iota(jnp.int32, (scen, width), 1) + first_link
    for half in range(fail_ref.shape[1] // width):
        ids = fail_ref[:, half * width : (half + 1) * width]

        def strike(_, state):
            ids, *alive = state
            for f in range(8):
                struck = jnp.broadcast_to(ids[:, f : f + 1], (scen, width))
                alive = [
                    jnp.where(struck == lane + b * width, 0.0, alive[b]) for b in range(link_here)
                ]
            return (pltpu.roll(ids, width - 8, 1), *alive)

        if half == 0:
            alive = [jnp.ones((scen, width), jnp.float32) for _ in range(link_here)]
        _, *alive = lax.fori_loop(0, width // 8, strike, (ids, *alive))
    for b in range(link_here):
        bound[b] = cap_ref[b : b + 1, :] * alive[b]
        dual_now[b] = dual_ref[b]

    peers(lambda peer: sel_way(peer, peer).wait_recv(), far_first=False)
    peers(lambda peer: sel_way(peer, peer).wait_send())

    def give(dst, index, peer):
        choice = all_sel[peer, pl.ds(me, 1), :]
        picked = dual_now[0]
        for b in range(1, link_here):
            picked = jnp.where(choice == b, dual_now[b], picked)
        dst[index] = picked.astype(jnp.bfloat16)

    def weights(base, c, i, h):
        rows = []
        for r in range(2):
            row = [
                tiles[inv_ref[base + 2 * h + q, c * CHUNK + 2 * i + r]] for q in range(2)
            ]
            rows.append(jnp.concatenate(row, axis=1))
        return jnp.concatenate(rows, axis=0)

    def weights_turned(base, c, i, h):
        rows = []
        for q in range(2):
            row = [
                turned[inv_ref[base + 2 * h + q, c * CHUNK + 2 * i + r]] for r in range(2)
            ]
            rows.append(jnp.concatenate(row, axis=1))
        return jnp.concatenate(rows, axis=0)

    def turn(k, _):
        for i in range(PIECES * 4):
            turned[k * PIECES * 4 + i] = tiles[k * PIECES * 4 + i].T
        return 0

    def backward():
        def quad(g, _):
            base = mix(my_group, g, groups) * QUAD
            for i in range(QUAD):

                @pl.when(base + i != me)
                def _():
                    arrival(*dual_ways, base + i).wait_recv()

            def chunk(c, _):
                pairs = [
                    jnp.concatenate([recv_dual[base + 2 * h], recv_dual[base + 2 * h + 1]], axis=1)
                    for h in range(QUAD // 2)
                ]
                for i in range(CHUNK // 2):
                    total = push[c, :, 2 * i * width : 2 * (i + 1) * width]
                    for h in range(QUAD // 2):
                        total = total + jnp.dot(
                            pairs[h],
                            weights_turned(base, c, i, h),
                            preferred_element_type=jnp.float32,
                        )
                    push[c, :, 2 * i * width : 2 * (i + 1) * width] = total
                return 0

            return lax.fori_loop(0, chunks, chunk, 0)

        push[...] = jnp.zeros(push.shape, push.dtype)
        lax.fori_loop(0, groups, quad, 0)

    def primal(t):
        def block(c, _):
            for i in range(CHUNK):
                b = c * CHUNK + i
                side = slice(i * width, (i + 1) * width)
                now = flow[b]
                price = cost_ref[pl.ds(b, 1), :] + push[c, :, side]
                raw = now - primal_step * price
                new = jnp.clip(raw, 0.0, upper_ref[pl.ds(b, 1), :])
                bar[c, :, side] = (2.0 * new - now).astype(jnp.bfloat16)
                flow[b] = jnp.where(t == ITERS - 1, raw, new)
            return 0

        lax.fori_loop(0, chunks, block, 0)

    def encode(load):
        peak = jnp.max(jnp.abs(load), axis=0, keepdims=True)
        power = jnp.ceil(jnp.log2(jnp.maximum(peak, 1e-30)))
        level = jnp.floor(load * (LEVELS * jnp.exp2(-power)) + 0.5)
        power = jnp.broadcast_to(power, (16, load.shape[1]))
        rows = jnp.concatenate([level, power], axis=0)
        return rows.astype(jnp.int32).astype(jnp.int16)

    def decode(coded):
        rows = coded.astype(jnp.int32).astype(jnp.float32)
        return rows[:scen] * (jnp.exp2(rows[scen : scen + 1]) * (1.0 / LEVELS))

    def forward():
        def quad(g, _):
            base = mix(my_group, groups - 1 - g, groups) * QUAD

            def chunk(c, totals):
                done = []
                for h in range(QUAD // 2):
                    total = totals[h]
                    for i in range(CHUNK // 2):
                        total = total + jnp.dot(
                            bar[c, :, 2 * i * width : 2 * (i + 1) * width],
                            weights(base, c, i, h),
                            preferred_element_type=jnp.float32,
                        )
                    done.append(total)
                return tuple(done)

            zero = jnp.zeros((scen, 2 * width), jnp.float32)
            totals = (zero,) * (QUAD // 2)
            if chunks == 1:
                totals = chunk(0, totals)
            else:
                totals = lax.fori_loop(0, chunks, chunk, totals)
            for h in range(QUAD // 2):
                coded = encode(totals[h])
                for q in range(2):
                    owner = base + 2 * h + q
                    load = coded[:, q * width : (q + 1) * width]
                    send_part[owner] = load

                    @pl.when(owner != me)
                    def _():
                        remote(*part_ways, owner).start()

            return 0

        lax.fori_loop(0, groups, quad, 0)

    def dual_step_all():
        def add(g, loads):
            base = mix(my_group, groups - 1 - g, groups) * QUAD
            for i in range(QUAD):

                @pl.when(base + i != me)
                def _():
                    arrival(*part_ways, base + i).wait_recv()

            for i in range(QUAD):
                part = decode(recv_part[base + i])
                choice = all_sel[base + i, pl.ds(me, 1), :]
                loads = tuple(
                    loads[b] + jnp.where(choice == b, part, 0.0) for b in range(link_here)
                )
            return loads

        zero = jnp.zeros((scen, width), jnp.float32)
        recv_part[me] = send_part[me]
        loads = lax.fori_loop(0, groups, add, (zero,) * link_here)
        for b in range(link_here):
            raw = dual_now[b] + dual_step * (loads[b] - bound[b])
            dual_out[b] = raw
            dual_now[b] = jnp.maximum(0.0, raw)

    save_flow = pltpu.make_async_copy(flow, flow_out, flow_sem)

    def phase(t, _):
        def offer(peer):
            give(send_dual, peer, peer)
            remote(*dual_ways, peer).start()

        peers(offer, far_first=False)
        give(recv_dual, me, me)

        @pl.when(t == 0)
        def _():
            for i in range(load_parts):
                load_tiles(i).wait()
            load_flow.wait()
            load_inv.wait()
            lax.fori_loop(0, tile_total // (PIECES * 4), turn, 0)

        backward()
        peers(lambda peer: arrival(*dual_ways, peer).wait_send())

        @pl.when(t < ITERS)
        def _():
            primal(t)

            @pl.when(t == ITERS - 1)
            def _():
                save_flow.start()

            forward()
            dual_step_all()
            peers(lambda peer: arrival(*part_ways, peer).wait_send())

        return 0

    lax.fori_loop(0, ITERS + 1, phase, 0)
    save_flow.wait()

    share = blocks // PIECES
    saves = []
    for k in range(PIECES):
        for b in range(k * share, (k + 1) * share):
            i = b % CHUNK
            flow[b] = push[b // CHUNK, :, i * width : (i + 1) * width]
        part = pl.ds(k * share, share)
        saves.append(pltpu.make_async_copy(flow.at[part], rc_out.at[part], out_sem.at[k]))
        saves[-1].start()
    for copy in saves:
        copy.wait()


def body(
    tile_values,
    link_of_tile,
    tile_count,
    fail_links,
    flow_start,
    dual_start,
    path_cost,
    path_upper,
    link_capacity,
):
    devs = lax.axis_size("path")
    blocks, slots, width, _ = tile_values.shape
    link_here, scen, _ = dual_start.shape
    tile_total = blocks * slots
    lanes = -(-blocks // 128) * 128
    chunks = blocks // CHUNK
    vmem = pl.BlockSpec(memory_space=pltpu.VMEM)
    anywhere = pl.BlockSpec(memory_space=pl.ANY)
    dma = pltpu.SemaphoreType.DMA
    dual_raw, flow_raw, pushed = pl.pallas_call(
        functools.partial(kernel, devs),
        out_shape=(
            jax.ShapeDtypeStruct(dual_start.shape, jnp.float32),
            jax.ShapeDtypeStruct(flow_start.shape, jnp.float32),
            jax.ShapeDtypeStruct(flow_start.shape, jnp.float32),
        ),
        in_specs=[pl.BlockSpec(memory_space=pltpu.HBM)] * 9,
        out_specs=(vmem, anywhere, anywhere),
        scratch_shapes=[
            pltpu.SMEM((devs, lanes), jnp.int32),
            pltpu.VMEM((slots, blocks), jnp.int32),
            pltpu.VMEM((1, blocks), jnp.int32),
            pltpu.VMEM((devs, lanes), jnp.int32),
            pltpu.VMEM((devs, width), jnp.int32),
            pltpu.VMEM((devs, devs, width), jnp.int32),
            pltpu.VMEM(fail_links.shape, jnp.int32),
            pltpu.VMEM(dual_start.shape, jnp.float32),
            pltpu.VMEM(path_cost.shape, jnp.float32),
            pltpu.VMEM(path_upper.shape, jnp.float32),
            pltpu.VMEM(link_capacity.shape, jnp.float32),
            dma((7,)),
            dma(()),
            pltpu.VMEM((tile_total + 1, width, width), jnp.bfloat16),
            pltpu.VMEM((tile_total + 1, width, width), jnp.bfloat16),
            pltpu.VMEM(flow_start.shape, jnp.float32),
            pltpu.VMEM((chunks, scen, CHUNK * width), jnp.float32),
            pltpu.VMEM((chunks, scen, CHUNK * width), jnp.bfloat16),
            pltpu.VMEM(dual_start.shape, jnp.float32),
            pltpu.VMEM(dual_start.shape, jnp.float32),
            pltpu.VMEM((devs, scen, width), jnp.bfloat16),
            pltpu.VMEM((devs, scen, width), jnp.bfloat16),
            pltpu.VMEM((devs, scen + 16, width), jnp.int16),
            pltpu.VMEM((devs, scen + 16, width), jnp.int16),
            dma((4,)),
            dma(()),
            dma((PIECES,)),
            dma((devs,)),
            dma((devs,)),
            dma((devs,)),
            dma((devs,)),
            dma((devs,)),
            dma((devs,)),
        ],
        compiler_params=pltpu.CompilerParams(
            collective_id=0, has_side_effects=True, vmem_limit_bytes=60 * 1024 * 1024
        ),
    )(
        link_of_tile.T,
        tile_count.reshape(1, blocks),
        fail_links,
        dual_start,
        path_cost,
        path_upper,
        link_capacity,
        tile_values.reshape(tile_total, width, width),
        flow_start,
    )
    flow_final = jnp.clip(flow_raw, 0.0, path_upper[:, None, :])
    return flow_final, jnp.maximum(0.0, dual_raw), path_cost[:, None, :] + pushed


def solution(mesh):
    rows = ("groups", "path")
    in_specs = (
        P(rows, None, None, None),
        P(rows, None),
        P(rows),
        P("groups", None),
        P(rows, None, None),
        P(rows, None, None),
        P(rows, None),
        P(rows, None),
        P(rows, None),
    )
    out_specs = (P(rows, None, None), P(rows, None, None), P(rows, None, None))
    return jax.shard_map(body, mesh=mesh, in_specs=in_specs, out_specs=out_specs, check_vma=False)
```

```python
import functools

import jax
import jax.numpy as jnp
from jax import lax
from jax.experimental import pallas as pl
from jax.experimental.pallas import tpu as pltpu
from jax.sharding import PartitionSpec as P

ITERS = 2
QUAD = 4
CHUNK = 32
LEVELS = 32000.0
PIECES = 4

primal_step = 0.5
dual_step = 0.25


def mix(a, b, count):
    if count & (count - 1):
        return lax.rem(a + b, count)
    total = 0
    bit = 1
    while bit < count:
        total = total + ((a // bit + b // bit) % 2) * bit
        bit *= 2
    return total


def kernel(
    devs,
    link_hbm,
    count_hbm,
    fail_hbm,
    dual_hbm,
    cost_hbm,
    upper_hbm,
    cap_hbm,
    tiles_hbm,
    flow_hbm,
    dual_out,
    flow_out,
    rc_out,
    inv_ref,
    link_ref,
    count_ref,
    inv_vec,
    sel_vec,
    all_sel,
    fail_ref,
    dual_ref,
    cost_ref,
    upper_ref,
    cap_ref,
    small_sem,
    inv_sem,
    tiles,
    turned,
    flow,
    push,
    bar,
    bound,
    dual_now,
    send_dual,
    recv_dual,
    send_part,
    recv_part,
    tile_sem,
    flow_sem,
    out_sem,
    sel_send,
    sel_recv,
    dual_send,
    dual_recv,
    part_send,
    part_recv,
):
    me = lax.axis_index("path")
    groups = devs // QUAD
    my_group = me // QUAD
    link_here, scen, width = dual_ref.shape
    tile_total = tiles.shape[0] - 1
    blocks = flow.shape[0]
    chunks = blocks // CHUNK
    load_parts = 4
    piece = tile_total // load_parts

    def load_tiles(i):
        part = pl.ds(i * piece, piece)
        return pltpu.make_async_copy(tiles_hbm.at[part], tiles.at[part], tile_sem.at[i])

    small = [
        pltpu.make_async_copy(src, dst, small_sem.at[i])
        for i, (src, dst) in enumerate(
            (
                (link_hbm, link_ref),
                (count_hbm, count_ref),
                (dual_hbm, dual_ref),
                (fail_hbm, fail_ref),
                (cap_hbm, cap_ref),
                (cost_hbm, cost_ref),
                (upper_hbm, upper_ref),
            )
        )
    ]
    for copy in small:
        copy.start()
    for i in range(load_parts):
        load_tiles(i).start()
    load_flow = pltpu.make_async_copy(flow_hbm, flow, flow_sem)
    load_flow.start()

    def remote(src, dst, send, recv, peer):
        return pltpu.make_async_remote_copy(
            src_ref=src.at[peer],
            dst_ref=dst.at[me],
            send_sem=send.at[peer],
            recv_sem=recv.at[me],
            device_id={"path": peer},
            device_id_type=pl.DeviceIdType.MESH,
        )

    def arrival(src, dst, send, recv, peer):
        return pltpu.make_async_remote_copy(
            src_ref=src.at[peer],
            dst_ref=dst.at[peer],
            send_sem=send.at[peer],
            recv_sem=recv.at[peer],
            device_id={"path": peer},
            device_id_type=pl.DeviceIdType.MESH,
        )

    def sel_way(peer, slot):
        return pltpu.make_async_remote_copy(
            src_ref=sel_vec,
            dst_ref=all_sel.at[slot],
            send_sem=sel_send.at[peer],
            recv_sem=sel_recv.at[slot],
            device_id={"path": peer},
            device_id_type=pl.DeviceIdType.MESH,
        )

    dual_ways = (send_dual, recv_dual, dual_send, dual_recv)
    part_ways = (send_part, recv_part, part_send, part_recv)

    def peers(step, far_first=True):
        def one(g, _):
            base = mix(my_group, groups - 1 - g if far_first else g, groups) * QUAD
            for i in range(QUAD):
                peer = base + i

                @pl.when(peer != me)
                def _():
                    step(peer)

            return 0

        lax.fori_loop(0, groups, one, 0)

    barrier = pltpu.get_barrier_semaphore()

    def greet(peer):
        pl.semaphore_signal(
            barrier, inc=1, device_id={"path": peer}, device_id_type=pl.DeviceIdType.MESH
        )

    peers(greet)
    for copy in small:
        copy.wait()

    slots = link_ref.shape[0]
    grid = (devs, blocks)
    first_slot = lax.broadcasted_iota(jnp.int32, grid, 1) * slots
    owner_link = lax.broadcasted_iota(jnp.int32, grid, 0) * link_here
    count = jnp.broadcast_to(count_ref[...], grid)
    place = jnp.full(grid, tile_total, jnp.int32)
    wanted = jnp.zeros(grid, jnp.int32)
    for k in range(slots):
        offset = jnp.broadcast_to(link_ref[k : k + 1, :], grid) - owner_link
        hit = (offset >= 0) & (offset < link_here) & (count > k)
        place = jnp.where(hit, first_slot + k, place)
        wanted = jnp.where(hit, offset, wanted)
    inv_vec[...] = jnp.zeros(inv_vec.shape, jnp.int32)
    inv_vec[:, :blocks] = place
    load_inv = pltpu.make_async_copy(inv_vec, inv_ref, inv_sem)
    load_inv.start()
    sel_vec[...] = jnp.broadcast_to(jnp.max(wanted, axis=1, keepdims=True), sel_vec.shape)
    all_sel[me] = sel_vec[...]
    pl.semaphore_wait(barrier, devs - 1)

    peers(lambda peer: sel_way(peer, me).start())

    tiles[tile_total] = jnp.zeros((width, width), tiles.dtype)
    turned[tile_total] = jnp.zeros((width, width), tiles.dtype)
    first_link = me * (link_here * width)
    lane = lax.broadcasted_iota(jnp.int32, (scen, width), 1) + first_link
    for half in range(fail_ref.shape[1] // width):
        ids = fail_ref[:, half * width : (half + 1) * width]

        def strike(_, state):
            ids, *alive = state
            for f in range(8):
                struck = jnp.broadcast_to(ids[:, f : f + 1], (scen, width))
                alive = [
                    jnp.where(struck == lane + b * width, 0.0, alive[b]) for b in range(link_here)
                ]
            return (pltpu.roll(ids, width - 8, 1), *alive)

        if half == 0:
            alive = [jnp.ones((scen, width), jnp.float32) for _ in range(link_here)]
        _, *alive = lax.fori_loop(0, width // 8, strike, (ids, *alive))
    for b in range(link_here):
        bound[b] = cap_ref[b : b + 1, :] * alive[b]
        dual_now[b] = dual_ref[b]

    peers(lambda peer: sel_way(peer, peer).wait_recv(), far_first=False)

    def give(dst, index, peer):
        choice = all_sel[peer, pl.ds(me, 1), :]
        picked = dual_now[0]
        for b in range(1, link_here):
            picked = jnp.where(choice == b, dual_now[b], picked)
        dst[index] = picked.astype(jnp.bfloat16)

    def weights(base, c, i, h):
        rows = []
        for r in range(2):
            row = [
                tiles[inv_ref[base + 2 * h + q, c * CHUNK + 2 * i + r]] for q in range(2)
            ]
            rows.append(jnp.concatenate(row, axis=1))
        return jnp.concatenate(rows, axis=0)

    def weights_turned(base, c, i, h):
        rows = []
        for q in range(2):
            row = [
                turned[inv_ref[base + 2 * h + q, c * CHUNK + 2 * i + r]] for r in range(2)
            ]
            rows.append(jnp.concatenate(row, axis=1))
        return jnp.concatenate(rows, axis=0)

    def turn(k, _):
        for i in range(PIECES * 4):
            turned[k * PIECES * 4 + i] = tiles[k * PIECES * 4 + i].T
        return 0

    def backward():
        def quad(g, _):
            base = mix(my_group, g, groups) * QUAD
            for i in range(QUAD):

                @pl.when(base + i != me)
                def _():
                    arrival(*dual_ways, base + i).wait_recv()

            def chunk(c, _):
                pairs = [
                    jnp.concatenate([recv_dual[base + 2 * h], recv_dual[base + 2 * h + 1]], axis=1)
                    for h in range(QUAD // 2)
                ]
                for i in range(CHUNK // 2):
                    total = push[c, :, 2 * i * width : 2 * (i + 1) * width]
                    for h in range(QUAD // 2):
                        total = total + jnp.dot(
                            pairs[h],
                            weights_turned(base, c, i, h),
                            preferred_element_type=jnp.float32,
                        )
                    push[c, :, 2 * i * width : 2 * (i + 1) * width] = total
                return 0

            return lax.fori_loop(0, chunks, chunk, 0)

        push[...] = jnp.zeros(push.shape, push.dtype)
        lax.fori_loop(0, groups, quad, 0)

    def primal(t):
        def block(c, _):
            for i in range(CHUNK):
                b = c * CHUNK + i
                side = slice(i * width, (i + 1) * width)
                now = flow[b]
                price = cost_ref[pl.ds(b, 1), :] + push[c, :, side]
                raw = now - primal_step * price
                new = jnp.clip(raw, 0.0, upper_ref[pl.ds(b, 1), :])
                bar[c, :, side] = (2.0 * new - now).astype(jnp.bfloat16)
                flow[b] = jnp.where(t == ITERS - 1, raw, new)
            return 0

        lax.fori_loop(0, chunks, block, 0)

    def encode(load):
        peak = jnp.max(jnp.abs(load), axis=0, keepdims=True)
        power = jnp.ceil(jnp.log2(jnp.maximum(peak, 1e-30)))
        level = jnp.floor(load * (LEVELS * jnp.exp2(-power)) + 0.5)
        power = jnp.broadcast_to(power, (16, load.shape[1]))
        rows = jnp.concatenate([level, power], axis=0)
        return rows.astype(jnp.int32).astype(jnp.int16)

    def decode(coded):
        rows = coded.astype(jnp.int32).astype(jnp.float32)
        return rows[:scen] * (jnp.exp2(rows[scen : scen + 1]) * (1.0 / LEVELS))

    def forward():
        def quad(g, _):
            base = mix(my_group, groups - 1 - g, groups) * QUAD

            def chunk(c, totals):
                done = []
                for h in range(QUAD // 2):
                    total = totals[h]
                    for i in range(CHUNK // 2):
                        total = total + jnp.dot(
                            bar[c, :, 2 * i * width : 2 * (i + 1) * width],
                            weights(base, c, i, h),
                            preferred_element_type=jnp.float32,
                        )
                    done.append(total)
                return tuple(done)

            zero = jnp.zeros((scen, 2 * width), jnp.float32)
            totals = (zero,) * (QUAD // 2)
            if chunks == 1:
                totals = chunk(0, totals)
            else:
                totals = lax.fori_loop(0, chunks, chunk, totals)
            for h in range(QUAD // 2):
                coded = encode(totals[h])
                for q in range(2):
                    owner = base + 2 * h + q
                    load = coded[:, q * width : (q + 1) * width]
                    send_part[owner] = load

                    @pl.when(owner != me)
                    def _():
                        remote(*part_ways, owner).start()

            return 0

        lax.fori_loop(0, groups, quad, 0)

    def dual_step_all():
        def add(g, loads):
            base = mix(my_group, groups - 1 - g, groups) * QUAD
            for i in range(QUAD):

                @pl.when(base + i != me)
                def _():
                    arrival(*part_ways, base + i).wait_recv()

            for i in range(QUAD):
                part = decode(recv_part[base + i])
                choice = all_sel[base + i, pl.ds(me, 1), :]
                loads = tuple(
                    loads[b] + jnp.where(choice == b, part, 0.0) for b in range(link_here)
                )
            return loads

        zero = jnp.zeros((scen, width), jnp.float32)
        recv_part[me] = send_part[me]
        loads = lax.fori_loop(0, groups, add, (zero,) * link_here)
        for b in range(link_here):
            raw = dual_now[b] + dual_step * (loads[b] - bound[b])
            dual_out[b] = raw
            dual_now[b] = jnp.maximum(0.0, raw)

    save_flow = pltpu.make_async_copy(flow, flow_out, flow_sem)

    def phase(t, _):
        def offer(peer):
            give(send_dual, peer, peer)
            remote(*dual_ways, peer).start()

        peers(offer, far_first=False)
        give(recv_dual, me, me)

        @pl.when(t > 0)
        def _():
            peers(lambda peer: arrival(*part_ways, peer).wait_send())

        @pl.when(t == 0)
        def _():
            peers(lambda peer: sel_way(peer, peer).wait_send())
            for i in range(load_parts):
                load_tiles(i).wait()
            load_flow.wait()
            load_inv.wait()
            lax.fori_loop(0, tile_total // (PIECES * 4), turn, 0)

        backward()

        @pl.when(t < ITERS)
        def _():
            primal(t)

            @pl.when(t == ITERS - 1)
            def _():
                save_flow.start()

            forward()
            peers(lambda peer: arrival(*dual_ways, peer).wait_send())
            dual_step_all()

        @pl.when(t == ITERS)
        def _():
            peers(lambda peer: arrival(*dual_ways, peer).wait_send())

        return 0

    lax.fori_loop(0, ITERS + 1, phase, 0)
    save_flow.wait()

    share = blocks // PIECES
    saves = []
    for k in range(PIECES):
        for b in range(k * share, (k + 1) * share):
            i = b % CHUNK
            flow[b] = push[b // CHUNK, :, i * width : (i + 1) * width]
        part = pl.ds(k * share, share)
        saves.append(pltpu.make_async_copy(flow.at[part], rc_out.at[part], out_sem.at[k]))
        saves[-1].start()
    for copy in saves:
        copy.wait()


def body(
    tile_values,
    link_of_tile,
    tile_count,
    fail_links,
    flow_start,
    dual_start,
    path_cost,
    path_upper,
    link_capacity,
):
    devs = lax.axis_size("path")
    blocks, slots, width, _ = tile_values.shape
    link_here, scen, _ = dual_start.shape
    tile_total = blocks * slots
    lanes = -(-blocks // 128) * 128
    chunks = blocks // CHUNK
    vmem = pl.BlockSpec(memory_space=pltpu.VMEM)
    anywhere = pl.BlockSpec(memory_space=pl.ANY)
    dma = pltpu.SemaphoreType.DMA
    dual_raw, flow_raw, pushed = pl.pallas_call(
        functools.partial(kernel, devs),
        out_shape=(
            jax.ShapeDtypeStruct(dual_start.shape, jnp.float32),
            jax.ShapeDtypeStruct(flow_start.shape, jnp.float32),
            jax.ShapeDtypeStruct(flow_start.shape, jnp.float32),
        ),
        in_specs=[pl.BlockSpec(memory_space=pltpu.HBM)] * 9,
        out_specs=(vmem, anywhere, anywhere),
        scratch_shapes=[
            pltpu.SMEM((devs, lanes), jnp.int32),
            pltpu.VMEM((slots, blocks), jnp.int32),
            pltpu.VMEM((1, blocks), jnp.int32),
            pltpu.VMEM((devs, lanes), jnp.int32),
            pltpu.VMEM((devs, width), jnp.int32),
            pltpu.VMEM((devs, devs, width), jnp.int32),
            pltpu.VMEM(fail_links.shape, jnp.int32),
            pltpu.VMEM(dual_start.shape, jnp.float32),
            pltpu.VMEM(path_cost.shape, jnp.float32),
            pltpu.VMEM(path_upper.shape, jnp.float32),
            pltpu.VMEM(link_capacity.shape, jnp.float32),
            dma((7,)),
            dma(()),
            pltpu.VMEM((tile_total + 1, width, width), jnp.bfloat16),
            pltpu.VMEM((tile_total + 1, width, width), jnp.bfloat16),
            pltpu.VMEM(flow_start.shape, jnp.float32),
            pltpu.VMEM((chunks, scen, CHUNK * width), jnp.float32),
            pltpu.VMEM((chunks, scen, CHUNK * width), jnp.bfloat16),
            pltpu.VMEM(dual_start.shape, jnp.float32),
            pltpu.VMEM(dual_start.shape, jnp.float32),
            pltpu.VMEM((devs, scen, width), jnp.bfloat16),
            pltpu.VMEM((devs, scen, width), jnp.bfloat16),
            pltpu.VMEM((devs, scen + 16, width), jnp.int16),
            pltpu.VMEM((devs, scen + 16, width), jnp.int16),
            dma((4,)),
            dma(()),
            dma((PIECES,)),
            dma((devs,)),
            dma((devs,)),
            dma((devs,)),
            dma((devs,)),
            dma((devs,)),
            dma((devs,)),
        ],
        compiler_params=pltpu.CompilerParams(
            collective_id=0, has_side_effects=True, vmem_limit_bytes=60 * 1024 * 1024
        ),
    )(
        link_of_tile.T,
        tile_count.reshape(1, blocks),
        fail_links,
        dual_start,
        path_cost,
        path_upper,
        link_capacity,
        tile_values.reshape(tile_total, width, width),
        flow_start,
    )
    flow_final = jnp.clip(flow_raw, 0.0, path_upper[:, None, :])
    return flow_final, jnp.maximum(0.0, dual_raw), path_cost[:, None, :] + pushed


def solution(mesh):
    rows = ("groups", "path")
    in_specs = (
        P(rows, None, None, None),
        P(rows, None),
        P(rows),
        P("groups", None),
        P(rows, None, None),
        P(rows, None, None),
        P(rows, None),
        P(rows, None),
        P(rows, None),
    )
    out_specs = (P(rows, None, None), P(rows, None, None), P(rows, None, None))
    return jax.shard_map(body, mesh=mesh, in_specs=in_specs, out_specs=out_specs, check_vma=False)
```
